32 devices in a mesh: dp: 4 (over x, core), ctx: 8 (over z, y).
Axes of the slice: x: 2, y: 2, z: 4, core: 2. Of those that a mesh axis runs over, the one named last changes fastest.
Arguments:
- query: bfloat16 [4, 1024, 8192], P('dp', 'ctx'), may hold values from -10 to 10
- key: bfloat16 [4, 1024, 1024], P('dp', 'ctx'), may hold values from -16 to 16
- value: bfloat16 [4, 1024, 1024], P('dp', 'ctx'), may hold values from -6 to 6
- out_grad: bfloat16 [4, 1024, 8192], P('dp', 'ctx'), may hold values from -6 to 6
- loss_mask: int32 [4, 1024], P('dp', 'ctx'), may hold values from 0 to 1, as said below
Outputs:
- attended: bfloat16 [4, 1024, 8192], P('dp', 'ctx')
- query_grad: bfloat16 [4, 1024, 8192], P('dp', 'ctx')
- key_grad: bfloat16 [4, 1024, 1024], P('dp', 'ctx')
- value_grad: bfloat16 [4, 1024, 1024], P('dp', 'ctx')
The draws below stay inside these ranges and needn't reach their ends.
Inputs may be any that keep to these rules, and one draw needn't show every extreme that they name: `loss_mask`: the last position of every sequence is 1.
All inputs are finite; a program needn't handle non-finite values.
Results may differ from the reference program's by a relative error of at most 0.015.
Values may be sent and summed in bfloat16 or wider, within the bound.
A program may use at most 128 MiB of HBM per device.

```python
import math
import jax
import jax.numpy as jnp
from jax import lax

QUERY_HEADS = 64
KEY_VALUE_HEADS = 8
HEAD_SIZE = 128
BATCH_SEQUENCES = 4
SEQUENCE_LENGTH = 1024


def draw_query(key, part):
    random_noise = jax.random.fold_in(key, 21)
    scale_factors = jnp.exp(jax.random.uniform(jax.random.fold_in(random_noise, 1), (BATCH_SEQUENCES, SEQUENCE_LENGTH, QUERY_HEADS, 1), minval=math.log(0.25), maxval=math.log(2.5)))
    base_offset = jnp.clip(jax.random.normal(jax.random.fold_in(random_noise, 2), (BATCH_SEQUENCES, SEQUENCE_LENGTH, QUERY_HEADS, HEAD_SIZE)), -4.0, 4.0)
    table_entries = base_offset * scale_factors
    return table_entries.reshape(BATCH_SEQUENCES, SEQUENCE_LENGTH, QUERY_HEADS * HEAD_SIZE).astype(jnp.bfloat16)


def draw_key(key, part):
    random_noise = jax.random.fold_in(key, 31)
    scale_factors = jnp.exp(jax.random.uniform(jax.random.fold_in(random_noise, 1), (BATCH_SEQUENCES, SEQUENCE_LENGTH, KEY_VALUE_HEADS, 1), minval=math.log(0.4), maxval=math.log(4.0)))
    base_offset = jnp.clip(jax.random.normal(jax.random.fold_in(random_noise, 2), (BATCH_SEQUENCES, SEQUENCE_LENGTH, KEY_VALUE_HEADS, HEAD_SIZE)), -4.0, 4.0)
    table_entries = base_offset * scale_factors
    return table_entries.reshape(BATCH_SEQUENCES, SEQUENCE_LENGTH, KEY_VALUE_HEADS * HEAD_SIZE).astype(jnp.bfloat16)


def draw_loss_mask(key, part):
    rank = jnp.arange(BATCH_SEQUENCES * SEQUENCE_LENGTH, dtype=jnp.int32).reshape(BATCH_SEQUENCES, SEQUENCE_LENGTH)
    threshold = 15 + 75 * rank // (BATCH_SEQUENCES * SEQUENCE_LENGTH)
    rolls = jax.random.randint(key, (BATCH_SEQUENCES, SEQUENCE_LENGTH), 0, 100)
    marked = jnp.where(rolls < threshold, 1, 0).astype(jnp.int32)
    final = jnp.arange(SEQUENCE_LENGTH, dtype=jnp.int32)[None, :] == SEQUENCE_LENGTH - 1
    return jnp.where(final, 1, marked).astype(jnp.int32)


def level_of(rng, shape, split, least, high):
    level = 1.0
    for axis_at, parts in split:
        heights = jax.random.uniform(jax.random.fold_in(jax.random.fold_in(rng, 6), axis_at), (parts,), jnp.float32, least / len(split), high / len(split))
        level = level * jnp.repeat(jnp.exp(heights), shape[axis_at] // parts).reshape((-1,) + (1,) * (len(shape) - 1 - axis_at))
    return level


def bell_draw(own_key, dims, scale, limit, split=(), held_as=jnp.bfloat16):
    drawn = jax.random.normal(own_key, dims, jnp.float32) * scale
    if len(split) > 0:
        drawn = level_of(own_key, dims, split, -0.22, 0.18) * drawn
    return jnp.clip(drawn, min=-limit, max=limit).astype(held_as)


def setup_inputs(seed: int = 0) -> dict:
    key_list = jax.random.split(jax.random.key(seed), 6)
    return {
        "query": draw_query(jax.random.fold_in(key_list[5], 71), 0),
        "key": draw_key(jax.random.fold_in(key_list[5], 71), 0),
        "value": bell_draw(key_list[2], (BATCH_SEQUENCES, SEQUENCE_LENGTH, KEY_VALUE_HEADS * HEAD_SIZE), 1.0, 6.0, ((0, 4), (1, 8))),
        "out_grad": bell_draw(key_list[3], (BATCH_SEQUENCES, SEQUENCE_LENGTH, QUERY_HEADS * HEAD_SIZE), 1.0, 6.0, ((0, 4), (1, 8))),
        "loss_mask": draw_loss_mask(jax.random.fold_in(key_list[5], 71), 0),
    }


def one_group(operands):
    queries, keys, values, grads = operands
    scale = 1.0 / math.sqrt(HEAD_SIZE)
    query_f = queries.astype(jnp.float32)
    key_f = keys.astype(jnp.float32)
    value_f = values.astype(jnp.float32)
    grad_f = grads.astype(jnp.float32)
    positions = jnp.arange(SEQUENCE_LENGTH)
    causal = positions[:, None] >= positions[None, :]
    scores = jnp.einsum('hqe,ke->hqk', query_f, key_f, precision=lax.Precision.HIGHEST) * scale
    scores = jnp.where(causal[None], scores, -jnp.inf)
    peak = lax.optimization_barrier(jnp.max(scores, axis=-1, keepdims=True))
    norm = peak + jnp.log(lax.optimization_barrier(jnp.sum(jnp.exp(scores - peak), axis=-1, keepdims=True)))
    probs = jnp.exp(scores - norm)
    weights = lax.optimization_barrier(probs.astype(jnp.bfloat16)).astype(jnp.float32)
    attended = lax.optimization_barrier(jnp.einsum('hqk,ke->hqe', weights, value_f, precision=lax.Precision.HIGHEST).astype(jnp.bfloat16))
    delta = lax.optimization_barrier(jnp.sum(grad_f * attended.astype(jnp.float32), axis=-1, keepdims=True))
    dots = jnp.einsum('hqe,ke->hqk', grad_f, value_f, precision=lax.Precision.HIGHEST)
    slopes = lax.optimization_barrier((probs * (dots - delta)).astype(jnp.bfloat16)).astype(jnp.float32)
    query_grad = (jnp.einsum('hqk,ke->hqe', slopes, key_f, precision=lax.Precision.HIGHEST) * scale).astype(jnp.bfloat16)
    key_grad = (jnp.einsum('hqk,hqe->ke', slopes, query_f, precision=lax.Precision.HIGHEST) * scale).astype(jnp.bfloat16)
    value_grad = jnp.einsum('hqk,hqe->ke', weights, grad_f, precision=lax.Precision.HIGHEST).astype(jnp.bfloat16)
    return (attended, query_grad, key_grad, value_grad)

def heads_first(input_array, count_of_heads):
    query_group_size = count_of_heads // KEY_VALUE_HEADS
    reshaped_input = input_array.reshape(BATCH_SEQUENCES, SEQUENCE_LENGTH, KEY_VALUE_HEADS, query_group_size, HEAD_SIZE).transpose(0, 2, 3, 1, 4)
    return reshaped_input.reshape(BATCH_SEQUENCES * KEY_VALUE_HEADS, query_group_size, SEQUENCE_LENGTH, HEAD_SIZE)

def kv_first(input_array):
    return input_array.reshape(BATCH_SEQUENCES, SEQUENCE_LENGTH, KEY_VALUE_HEADS, HEAD_SIZE).transpose(0, 2, 1, 3).reshape(BATCH_SEQUENCES * KEY_VALUE_HEADS, SEQUENCE_LENGTH, HEAD_SIZE)

def reference(query, key, value, out_grad, loss_mask):
    count = jnp.sum(loss_mask).astype(jnp.float32)
    factor = BATCH_SEQUENCES * SEQUENCE_LENGTH / count
    token_weight = loss_mask.astype(jnp.float32) * factor
    scaled = (out_grad.astype(jnp.float32) * token_weight[:, :, None]).astype(jnp.bfloat16)
    query_group_size = QUERY_HEADS // KEY_VALUE_HEADS
    results = lax.map(one_group, (heads_first(query, QUERY_HEADS), kv_first(key), kv_first(value), heads_first(scaled, QUERY_HEADS)))
    attended, query_grad, key_grad, value_grad = results

    def heads_back(input_array):
        return input_array.reshape(BATCH_SEQUENCES, KEY_VALUE_HEADS, query_group_size, SEQUENCE_LENGTH, HEAD_SIZE).transpose(0, 3, 1, 2, 4).reshape(BATCH_SEQUENCES, SEQUENCE_LENGTH, QUERY_HEADS * HEAD_SIZE)

    def kv_back(input_array):
        return input_array.reshape(BATCH_SEQUENCES, KEY_VALUE_HEADS, SEQUENCE_LENGTH, HEAD_SIZE).transpose(0, 2, 1, 3).reshape(BATCH_SEQUENCES, SEQUENCE_LENGTH, KEY_VALUE_HEADS * HEAD_SIZE)
    return (heads_back(attended), heads_back(query_grad), kv_back(key_grad), kv_back(value_grad))
```

```python
import functools
import math

import jax
import jax.numpy as jnp
from jax import lax
from jax.experimental import pallas as pl
from jax.experimental.pallas import tpu as pltpu
from jax.sharding import PartitionSpec as P

KEY_VALUE_HEADS = 8
HEAD_SIZE = 128
SCALE = 1.0 / math.sqrt(HEAD_SIZE)
LOG2E = math.log2(math.e)
NT = (((1,), (1,)), ((), ()))
NN = (((1,), (0,)), ((), ()))


def mm(a, b, dims=NN):
    return lax.dot_general(a, b, dims, preferred_element_type=jnp.float32)


def pair_rows(block):
    return jnp.concatenate([block[:, :HEAD_SIZE], block[:, HEAD_SIZE:]], 0)


def head_group(me, slots, rows, group, q_of, g_of, k_of, v_of, put_out, put_dq, s_ref, w_ref, x_ref, dk_ref, dv_ref):
    width = 2 * rows
    k_t = jnp.concatenate([k_of(s).T for s in range(slots)], 1)
    v_t = jnp.concatenate([v_of(s).T for s in range(slots)], 1)
    key_at = lax.broadcasted_iota(jnp.int32, (rows, width), 0)
    row_at = lax.broadcasted_iota(jnp.int32, (rows, width), 1) % rows
    tri = key_at <= row_at
    for pair in range(group // 2):
        q = pair_rows(q_of(pair))
        g = pair_rows(g_of(pair))
        top = None
        for s in range(slots):
            scores = mm(k_of(s), q, NT)
            if s == 0:
                scores = jnp.where(tri, scores, -1e30)
            s_ref[s * rows:(s + 1) * rows] = scores
            peak = jnp.max(scores, axis=0, keepdims=True)
            if s > 0:
                peak = jnp.where(s <= me, peak, -1e30)
            top = peak if top is None else jnp.maximum(top, peak)
        top = top * (SCALE * LOG2E)
        mass = None
        for s in range(slots):
            at = top if s == 0 else jnp.where(s <= me, top, 1e30)
            e = jnp.exp2(s_ref[s * rows:(s + 1) * rows] * (SCALE * LOG2E) - at)
            s_ref[s * rows:(s + 1) * rows] = e
            part = jnp.sum(e, axis=0, keepdims=True)
            mass = part if mass is None else mass + part
        inv = 1.0 / mass
        for s in range(slots):
            p = s_ref[s * rows:(s + 1) * rows] * inv
            w_ref[s * rows:(s + 1) * rows] = p.astype(jnp.bfloat16)
            s_ref[s * rows:(s + 1) * rows] = p
        out_t = mm(v_t, w_ref[...])
        out = out_t.T.astype(jnp.bfloat16)
        put_out(pair, out)
        prod = out.astype(jnp.float32) * g.astype(jnp.float32)
        delta = jnp.sum(prod.T, axis=0, keepdims=True)
        for s in range(slots):
            dots = mm(v_of(s), g, NT)
            x = (s_ref[s * rows:(s + 1) * rows] * (dots - delta)).astype(jnp.bfloat16)
            x_ref[s * rows:(s + 1) * rows] = x
        dv = mm(w_ref[...], g)
        dk = mm(x_ref[...], q)
        if pair == 0:
            dv_ref[...] = dv
            dk_ref[...] = dk
        else:
            dv_ref[...] += dv
            dk_ref[...] += dk
        put_dq(pair, mm(k_t, x_ref[...]).T)


def unpair(block, rows):
    return jnp.concatenate([block[:rows], block[rows:]], 1)


def compute_kernel(slots, rows, group, q_ref, g_ref, k_ref, v_ref, weight_ref, out_ref, dq_ref, dk_ref, dv_ref, s_ref, w_ref, x_ref, dk_acc, dv_acc):
    me = lax.axis_index("ctx")
    two = 2 * HEAD_SIZE

    def place(s):
        return pl.ds(pl.multiple_of(lax.rem(me + (slots - s), slots) * rows, rows), rows)

    def put_out(pair, out):
        out_ref[:, pair * two:(pair + 1) * two] = unpair(out, rows)

    def put_dq(pair, dq):
        dq_ref[:, pair * two:(pair + 1) * two] = unpair(dq * SCALE, rows).astype(jnp.bfloat16)

    head_group(
        me, slots, rows, group,
        lambda pair: q_ref[:, pair * two:(pair + 1) * two],
        lambda pair: (g_ref[:, pair * two:(pair + 1) * two].astype(jnp.float32) * weight_ref[...]).astype(jnp.bfloat16),
        lambda s: k_ref[place(s)],
        lambda s: v_ref[place(s)],
        put_out, put_dq, s_ref, w_ref, x_ref, dk_acc, dv_acc,
    )
    for s in range(slots):
        dk_ref[place(s)] = dk_acc[s * rows:(s + 1) * rows] * SCALE
        dv_ref[place(s)] = dv_acc[s * rows:(s + 1) * rows]


def body(query, key, value, out_grad, loss_mask):
    slots = lax.axis_size("ctx")
    rows = query.shape[1]
    group = query.shape[2] // key.shape[2]
    length = slots * rows
    all_tokens = query.shape[0] * length * lax.axis_size("dp")
    count = lax.psum(jnp.sum(loss_mask).astype(jnp.float32), ("dp", "ctx"))
    weight = (loss_mask[0].astype(jnp.float32) * (all_tokens / count))[:, None]
    kv = lax.all_gather(jnp.concatenate([key[0], value[0]], 1), "ctx", axis=0, tiled=False)
    kv = kv.reshape(length, -1)
    wide = group * HEAD_SIZE
    heads = KEY_VALUE_HEADS
    row_spec = pl.BlockSpec((rows, wide), lambda j: (0, j))
    key_spec = pl.BlockSpec((length, HEAD_SIZE), lambda j: (0, j))
    out, dq, dk, dv = pl.pallas_call(
        functools.partial(compute_kernel, slots, rows, group),
        grid=(heads,),
        in_specs=[
            row_spec, row_spec, key_spec,
            pl.BlockSpec((length, HEAD_SIZE), lambda j: (0, j + heads)),
            pl.BlockSpec((rows, 1), lambda j: (0, 0)),
        ],
        out_specs=[row_spec, row_spec, key_spec, key_spec],
        out_shape=[
            jax.ShapeDtypeStruct((rows, heads * wide), jnp.bfloat16),
            jax.ShapeDtypeStruct((rows, heads * wide), jnp.bfloat16),
            jax.ShapeDtypeStruct((length, heads * HEAD_SIZE), jnp.float32),
            jax.ShapeDtypeStruct((length, heads * HEAD_SIZE), jnp.float32),
        ],
        scratch_shapes=[
            pltpu.VMEM((length, 2 * rows), jnp.float32),
            pltpu.VMEM((length, 2 * rows), jnp.bfloat16),
            pltpu.VMEM((length, 2 * rows), jnp.bfloat16),
            pltpu.VMEM((length, HEAD_SIZE), jnp.float32),
            pltpu.VMEM((length, HEAD_SIZE), jnp.float32),
        ],
        compiler_params=pltpu.CompilerParams(vmem_limit_bytes=40 * 1024 * 1024),
    )(query[0], out_grad[0], kv, kv, weight)
    parts = jnp.concatenate([dk, dv], 1).reshape(slots, rows, -1)
    sums = lax.psum_scatter(parts, "ctx", scatter_dimension=0, tiled=False).astype(jnp.bfloat16)
    half = heads * HEAD_SIZE
    return (out[None], dq[None], sums[None, :, :half], sums[None, :, half:])


def solution(mesh):
    placed = P("dp", "ctx", None)
    return jax.shard_map(
        body,
        mesh=mesh,
        in_specs=(placed, placed, placed, placed, P("dp", "ctx")),
        out_specs=(placed, placed, placed, placed),
        check_vma=False,
    )
```

```python
import functools
import math

import jax
import jax.numpy as jnp
from jax import lax
from jax.experimental import pallas as pl
from jax.experimental.pallas import tpu as pltpu
from jax.sharding import PartitionSpec as P

KEY_VALUE_HEADS = 8
HEAD_SIZE = 128
SCALE = 1.0 / math.sqrt(HEAD_SIZE)
LOG2E = math.log2(math.e)
NT = (((1,), (1,)), ((), ()))
NN = (((1,), (0,)), ((), ()))


def mm(a, b, dims=NN):
    return lax.dot_general(a, b, dims, preferred_element_type=jnp.float32)


def pair_rows(block):
    return jnp.concatenate([block[:, :HEAD_SIZE], block[:, HEAD_SIZE:]], 0)


def head_group(me, slots, rows, group, q_of, g_of, k_of, v_of, put_out, put_dq, s_ref, w_ref, x_ref, dk_ref, dv_ref):
    width = 2 * rows
    k_t = jnp.concatenate([k_of(s).T for s in range(slots)], 1)
    v_t = jnp.concatenate([v_of(s).T for s in range(slots)], 1)
    key_at = lax.broadcasted_iota(jnp.int32, (rows, width), 0)
    row_at = lax.broadcasted_iota(jnp.int32, (rows, width), 1) % rows
    tri = key_at <= row_at
    for pair in range(group // 2):
        q = pair_rows(q_of(pair))
        g = pair_rows(g_of(pair))
        top = None
        for s in range(slots):
            scores = mm(k_of(s), q, NT)
            if s == 0:
                scores = jnp.where(tri, scores, -1e30)
            s_ref[s * rows:(s + 1) * rows] = scores
            peak = jnp.max(scores, axis=0, keepdims=True)
            if s > 0:
                peak = jnp.where(s <= me, peak, -1e30)
            top = peak if top is None else jnp.maximum(top, peak)
        top = top * (SCALE * LOG2E)
        mass = None
        for s in range(slots):
            at = top if s == 0 else jnp.where(s <= me, top, 1e30)
            e = jnp.exp2(s_ref[s * rows:(s + 1) * rows] * (SCALE * LOG2E) - at)
            s_ref[s * rows:(s + 1) * rows] = e
            part = jnp.sum(e, axis=0, keepdims=True)
            mass = part if mass is None else mass + part
        inv = 1.0 / mass
        for s in range(slots):
            p = s_ref[s * rows:(s + 1) * rows] * inv
            w_ref[s * rows:(s + 1) * rows] = p.astype(jnp.bfloat16)
            s_ref[s * rows:(s + 1) * rows] = p
        out_t = mm(v_t, w_ref[...])
        out = out_t.T.astype(jnp.bfloat16)
        put_out(pair, out)
        prod = out.astype(jnp.float32) * g.astype(jnp.float32)
        delta = jnp.sum(prod.T, axis=0, keepdims=True)
        for s in range(slots):
            dots = mm(v_of(s), g, NT)
            x = (s_ref[s * rows:(s + 1) * rows] * (dots - delta)).astype(jnp.bfloat16)
            x_ref[s * rows:(s + 1) * rows] = x
        dv = mm(w_ref[...], g)
        dk = mm(x_ref[...], q)
        if pair == 0:
            dv_ref[...] = dv
            dk_ref[...] = dk
        else:
            dv_ref[...] += dv
            dk_ref[...] += dk
        put_dq(pair, mm(k_t, x_ref[...]).T)


def unpair(block, rows):
    return jnp.concatenate([block[:rows], block[rows:]], 1)


def fused_kernel(
    slots, lines, copies, rows, group, heads, all_tokens,
    q_ref, g_ref, k_ref, v_ref, mask_ref, count_ref,
    out_ref, dq_ref, kv_ref,
    s_ref, w_ref, x_ref, dk_acc, dv_acc,
    stash, own, y_out, y_in, z_out, z_in, ctx_counts, dp_out, dp_counts, factor_ref,
    y_sent, y_got, z_sent, z_got, c_sent, c_got, d_sent, d_got,
):
    step = pl.program_id(0)
    me = lax.axis_index("ctx")
    batch = lax.axis_index("dp")
    depths = slots // lines
    depth, line = me // lines, lax.rem(me, lines)
    two = 2 * HEAD_SIZE

    def at_ctx(shift):
        return {"ctx": lax.rem(me + shift, slots)}

    def at_dp(shift):
        return {"dp": lax.rem(batch + shift, copies)}

    def count_copy(shift):
        return pltpu.make_async_remote_copy(
            src_ref=count_ref, dst_ref=ctx_counts.at[shift - 1],
            send_sem=c_sent.at[shift - 1], recv_sem=c_got.at[shift - 1],
            device_id=at_ctx(shift), device_id_type=pl.DeviceIdType.MESH)

    def total_copy(shift):
        return pltpu.make_async_remote_copy(
            src_ref=dp_out, dst_ref=dp_counts.at[shift - 1],
            send_sem=d_sent.at[shift - 1], recv_sem=d_got.at[shift - 1],
            device_id=at_dp(shift), device_id_type=pl.DeviceIdType.MESH)

    def y_copy(head, hop, back):
        return pltpu.make_async_remote_copy(
            src_ref=y_out.at[head, hop - 1, back], dst_ref=y_in.at[head, hop - 1, back],
            send_sem=y_sent.at[head, hop - 1, back], recv_sem=y_got.at[head, hop - 1, back],
            device_id={"ctx": depth * lines + lax.rem(line + hop, lines)},
            device_id_type=pl.DeviceIdType.MESH)

    def z_copy(head, back):
        return pltpu.make_async_remote_copy(
            src_ref=z_out.at[head, back - 1], dst_ref=z_in.at[head, back - 1],
            send_sem=z_sent.at[head, back - 1], recv_sem=z_got.at[head, back - 1],
            device_id={"ctx": lax.rem(me + slots - back * lines, slots)},
            device_id_type=pl.DeviceIdType.MESH)

    @pl.when(step == 0)
    def _():
        barrier = pltpu.get_barrier_semaphore()
        for shift in range(1, slots):
            pl.semaphore_signal(barrier, inc=1, device_id=at_ctx(shift), device_id_type=pl.DeviceIdType.MESH)
        for shift in range(1, copies):
            pl.semaphore_signal(barrier, inc=1, device_id=at_dp(shift), device_id_type=pl.DeviceIdType.MESH)
        pl.semaphore_wait(barrier, slots + copies - 2)
        for shift in range(1, slots):
            count_copy(shift).start()

    def place(s):
        return pl.ds(pl.multiple_of(lax.rem(me + (slots - s), slots) * rows, rows), rows)

    def put_out(pair, out):
        out_ref[:, pair * two:(pair + 1) * two] = unpair(out, rows)
        if pair == 0:
            @pl.when(step == 0)
            def _():
                total = count_ref[...]
                for shift in range(1, slots):
                    count_copy(shift).wait()
                    total = total + ctx_counts[shift - 1]
                dp_out[...] = total
                for shift in range(1, copies):
                    total_copy(shift).start()

    def put_dq(pair, dq):
        if pair == 0:
            @pl.when(step == 0)
            def _():
                total = dp_out[...]
                for shift in range(1, copies):
                    total_copy(shift).wait()
                    total = total + dp_counts[shift - 1]
                factor_ref[...] = all_tokens / total
        scaled = dq * SCALE * factor_ref[0:1, 0:1]
        dq_ref[:, pair * two:(pair + 1) * two] = unpair(scaled, rows).astype(jnp.bfloat16)

    mask = mask_ref[...]
    head_group(
        me, slots, rows, group,
        lambda pair: q_ref[:, pair * two:(pair + 1) * two],
        lambda pair: (g_ref[:, pair * two:(pair + 1) * two].astype(jnp.float32) * mask).astype(jnp.bfloat16),
        lambda s: k_ref[place(s)],
        lambda s: v_ref[place(s)],
        put_out, put_dq, s_ref, w_ref, x_ref, dk_acc, dv_acc,
    )

    def partial_at(device):
        s = lax.rem(me - device + slots, slots)
        where = pl.ds(pl.multiple_of(s * rows, rows), rows)
        return jnp.concatenate([dk_acc[where] * SCALE, dv_acc[where]], 1) * factor_ref[0:1, 0:1]

    def send_across(head):
        for back in range(depths):
            @pl.when(back <= depth)
            def _():
                for hop in range(1, lines):
                    other = (depth - back) * lines + lax.rem(line + hop, lines)
                    y_out[head, hop - 1, back] = partial_at(other).astype(jnp.bfloat16)
                    y_copy(head, hop, back).start()

    def send_down(head):
        for back in range(depths):
            @pl.when(back <= depth)
            def _():
                total = stash[back]
                for hop in range(1, lines):
                    y_copy(head, hop, back).wait()
                    total = total + y_in[head, hop - 1, back].astype(jnp.float32)
                if back == 0:
                    own[head] = total
                else:
                    z_out[head, back - 1] = total.astype(jnp.bfloat16)
                    z_copy(head, back).start()

    def keep():
        for back in range(depths):
            @pl.when(back <= depth)
            def _():
                stash[back] = partial_at(me - back * lines)

    send_across(step)

    @pl.when(step > 0)
    def _():
        send_down(step - 1)

    keep()

    @pl.when(step == heads - 1)
    def _():
        send_down(heads - 1)
        for head in range(heads):
            for back in range(1, depths):
                @pl.when(depth + back < depths)
                def _():
                    z_copy(head, back).wait_recv()
                    own[head] = own[head] + z_in[head, back - 1].astype(jnp.float32)

                @pl.when(back <= depth)
                def _():
                    z_copy(head, back).wait_send()
            total = own[head].astype(jnp.bfloat16)
            kv_ref[:, head * HEAD_SIZE:(head + 1) * HEAD_SIZE] = total[:, :HEAD_SIZE]
            kv_ref[:, (heads + head) * HEAD_SIZE:(heads + head + 1) * HEAD_SIZE] = total[:, HEAD_SIZE:]


def body(lines, query, key, value, out_grad, loss_mask):
    slots = lax.axis_size("ctx")
    copies = lax.axis_size("dp")
    depths = slots // lines
    rows = query.shape[1]
    group = query.shape[2] // key.shape[2]
    length = slots * rows
    all_tokens = float(query.shape[0] * length * copies)
    mask = loss_mask[0].astype(jnp.float32)
    count = jnp.broadcast_to(jnp.sum(mask), (8, HEAD_SIZE))
    kv = lax.all_gather(jnp.concatenate([key[0], value[0]], 1), "ctx", axis=0, tiled=True)
    wide = group * HEAD_SIZE
    heads = KEY_VALUE_HEADS
    two = 2 * HEAD_SIZE
    row_spec = pl.BlockSpec((rows, wide), lambda j: (0, j))
    whole = pl.BlockSpec(memory_space=pltpu.VMEM)
    wait = pltpu.SemaphoreType.DMA
    f32, b16 = jnp.float32, jnp.bfloat16
    out, dq, grads = pl.pallas_call(
        functools.partial(fused_kernel, slots, lines, copies, rows, group, heads, all_tokens),
        grid=(heads,),
        in_specs=[
            row_spec, row_spec,
            pl.BlockSpec((length, HEAD_SIZE), lambda j: (0, j)),
            pl.BlockSpec((length, HEAD_SIZE), lambda j: (0, j + heads)),
            whole, whole,
        ],
        out_specs=[row_spec, row_spec, whole],
        out_shape=[
            jax.ShapeDtypeStruct((rows, heads * wide), b16),
            jax.ShapeDtypeStruct((rows, heads * wide), b16),
            jax.ShapeDtypeStruct((rows, heads * two), b16),
        ],
        scratch_shapes=[
            pltpu.VMEM((length, 2 * rows), f32),
            pltpu.VMEM((length, 2 * rows), b16),
            pltpu.VMEM((length, 2 * rows), b16),
            pltpu.VMEM((length, HEAD_SIZE), f32),
            pltpu.VMEM((length, HEAD_SIZE), f32),
            pltpu.VMEM((depths, rows, two), f32),
            pltpu.VMEM((heads, rows, two), f32),
            pltpu.VMEM((heads, lines - 1, depths, rows, two), b16),
            pltpu.VMEM((heads, lines - 1, depths, rows, two), b16),
            pltpu.VMEM((heads, depths - 1, rows, two), b16),
            pltpu.VMEM((heads, depths - 1, rows, two), b16),
            pltpu.VMEM((slots - 1, 8, HEAD_SIZE), f32),
            pltpu.VMEM((8, HEAD_SIZE), f32),
            pltpu.VMEM((copies - 1, 8, HEAD_SIZE), f32),
            pltpu.VMEM((8, HEAD_SIZE), f32),
            wait((heads, lines - 1, depths)), wait((heads, lines - 1, depths)),
            wait((heads, depths - 1)), wait((heads, depths - 1)),
            wait((slots - 1,)), wait((slots - 1,)),
            wait((copies - 1,)), wait((copies - 1,)),
        ],
        compiler_params=pltpu.CompilerParams(
            vmem_limit_bytes=48 * 1024 * 1024, collective_id=0, has_side_effects=True),
    )(query[0], out_grad[0], kv, kv, mask[:, None], count)
    half = heads * HEAD_SIZE
    return (out[None], dq[None], grads[None, :, :half], grads[None, :, half:])


def solution(mesh):
    placed = P("dp", "ctx", None)
    lines = 2 if mesh.shape["ctx"] < 16 else 4
    return jax.shard_map(
        functools.partial(body, lines),
        mesh=mesh,
        in_specs=(placed, placed, placed, placed, P("dp", "ctx")),
        out_specs=(placed, placed, placed, placed),
        check_vma=False,
    )
```
